768 devices in a mesh: pair: 32 (over x, z_lo, core), virt: 24 (over z_hi, y).
Axes of the slice: x: 4, y: 8, z: 12 (z_hi: 3, z_lo: 4; z = z_hi * 4 + z_lo), core: 2. Of those that a mesh axis runs over, the one named last changes fastest.
Arguments:
- amplitudes: bfloat16 [32, 2, 2, 1536, 1536], P('pair', None, None, 'virt'), may hold values from -6 to 6
- integrals: bfloat16 [1536, 1536], P('virt', 'pair'), may hold values from -0.4375 to 0.4375
- irreps: int32 [1536], replicated, may hold values from 0 to 7, as said below
- occ_energy: float32 [64], replicated, may hold values from -2 to -0.4
- virt_energy: float32 [1536], replicated, may hold values from 0.2 to 3
Outputs:
- new_amplitudes: bfloat16 [32, 2, 2, 1536, 1536], P('pair', None, None, 'virt')
The draws below stay inside these ranges and needn't reach their ends.
Inputs may be any that keep to these rules, and one draw needn't show every extreme that they name: `irreps`: labels never decrease along the virtual orbitals (orbitals sorted by irrep).
All inputs are finite; a program needn't handle non-finite values.
Results may differ from the reference program's by a relative error of at most 0.0032.
Values may be sent and summed in bfloat16 or wider, within the bound.
No kernel may reach another device: no remote copies, remote signals or barrier semaphores. Data moves between devices by JAX's collectives and lax.ppermute only.
A program may use at most 32 MiB of HBM per device.

```python
import jax
import jax.numpy as jnp
from jax import lax

V = 1536
OB = 2
NIRREP = 8
PB = 32
OCC = 64


def draw_irreps(key, part):
    key = jax.random.fold_in(key, 11)
    cuts = jax.random.randint(key, (NIRREP - 1,), 1, V)
    position = jnp.arange(V, dtype=jnp.int32)
    return jnp.sum((position[:, None] >= cuts[None, :]).astype(jnp.int32), axis=1)


def level_of(stream_key, dims, shards, low, top_value):
    loudness = 1.0
    for dim, parts in shards:
        steps = jax.random.uniform(jax.random.fold_in(jax.random.fold_in(stream_key, 6), dim), (parts,), jnp.float32, low / len(shards), top_value / len(shards))
        loudness = loudness * jnp.repeat(jnp.exp(steps), dims[dim] // parts).reshape((-1,) + (1,) * (len(dims) - 1 - dim))
    return loudness


def scatter_about(key, shape, width, reach, split=(), kind=jnp.bfloat16):
    loudness = level_of(key, shape, split, -0.22, 0.18) if split else 1.0
    values = jax.random.normal(key, shape, jnp.float32) * width * loudness
    return jnp.minimum(jnp.maximum(values, -reach), reach).astype(kind)


def setup_inputs(seed: int = 0) -> dict:
    key_of = jax.random.split(jax.random.key(seed), 6)
    return {
        "amplitudes": scatter_about(key_of[0], (PB, OB, OB, V, V), 1.0, 6.0, ((0, 32), (3, 24))),
        "integrals": scatter_about(key_of[1], (V, V), (V // NIRREP) ** -0.5, 0.4375, ((0, 24), (1, 32))),
        "irreps": draw_irreps(jax.random.fold_in(key_of[5], 71), 0),
        "occ_energy": jnp.clip(jax.random.uniform(key_of[3], (OCC,), jnp.float32, -2.0, -0.4), -2.0, -0.4),
        "virt_energy": jnp.clip(jax.random.uniform(key_of[4], (V,), jnp.float32, 0.2, 3.0), 0.2, 3.0),
    }


def reference(amplitudes, integrals, irreps, occ_energy, virt_energy):
    same = irreps[:, None] == irreps[None, :]
    masked = jnp.where(same, integrals, jnp.zeros_like(integrals)).astype(jnp.float32)

    def one_block(block):
        return jnp.einsum("ac,ijbc->ijba", masked, block.astype(jnp.float32)).astype(jnp.bfloat16)

    cycle = lax.map(one_block, amplitudes)
    half = PB // 2

    def finish(index):
        partner = (index + half) % PB
        own = cycle[index].astype(jnp.float32)
        other = jnp.transpose(cycle[partner], (1, 0, 3, 2)).astype(jnp.float32)
        occ_i = lax.dynamic_slice_in_dim(occ_energy, (index * OB).astype(jnp.int32), OB)
        occ_j = lax.dynamic_slice_in_dim(occ_energy, (partner * OB).astype(jnp.int32), OB)
        denom = occ_i[:, None, None, None] + occ_j[None, :, None, None] - virt_energy[None, None, :, None] - virt_energy[None, None, None, :]
        return (amplitudes[index].astype(jnp.float32) + (own + other) / denom).astype(jnp.bfloat16)

    return lax.map(finish, jnp.arange(PB, dtype=jnp.int32))
```

```python
import jax
import jax.numpy as jnp
from jax import lax
from jax.sharding import Mesh, PartitionSpec as P

X, ZL, C = 4, 4, 2
ZH, Y = 3, 8
PAIR = ("x", "zl", "c")
VIRT = ("zh", "y")


def passed_along(value, axis, steps):
    count = lax.axis_size(axis)
    pairs = [(source, (source + steps) % count) for source in range(count)]
    return lax.ppermute(value, axis, pairs)


def spread(value, axis, count):
    copies = jnp.broadcast_to(value[None], (count,) + value.shape)
    return lax.all_to_all(copies, axis, split_axis=0, concat_axis=0, tiled=True)


def local(amplitudes, integrals, irreps, occ_energy, virt_energy):
    block = amplitudes[0]
    occ_block = block.shape[0]
    width = block.shape[2]
    virt_total = block.shape[3]
    flat = block.reshape(occ_block * occ_block * width, virt_total)
    npair = X * ZL * C
    nvirt = ZH * Y
    depth = integrals.shape[1]
    index = lax.axis_index(PAIR)
    place = lax.axis_index(VIRT)
    mirrored = passed_along(flat, "x", X // 2)

    irreps_a = lax.dynamic_slice_in_dim(irreps, place * width, width)
    irreps_c = lax.dynamic_slice_in_dim(irreps, index * depth, depth)
    keep = irreps_c[:, None] == irreps_a[None, :]
    masked = jnp.where(keep, integrals.T, jnp.zeros((), integrals.dtype))
    strip = spread(masked, VIRT, nvirt)
    strip = jnp.transpose(strip, (1, 0, 2)).reshape(depth, virt_total)
    strip = lax.all_gather(strip, "zl", axis=0, tiled=True)
    half = spread(strip, "x", X).reshape(X, ZL, depth, virt_total)
    other_half = passed_along(half, "c", 1)
    first = lax.axis_index("c") == 0
    whole = jnp.stack(
        [jnp.where(first, half, other_half), jnp.where(first, other_half, half)], axis=2
    ).reshape(virt_total, virt_total)

    turned = lax.dot_general(
        whole, mirrored, (((0,), (1,)), ((), ())), preferred_element_type=jnp.float32
    ).astype(jnp.bfloat16)
    arrived = lax.all_to_all(
        turned.reshape(nvirt, width, occ_block * occ_block * width),
        VIRT,
        split_axis=0,
        concat_axis=0,
        tiled=True,
    )
    own = jnp.dot(flat, whole, preferred_element_type=jnp.float32).astype(jnp.bfloat16)
    own = own.reshape(occ_block, occ_block, width, virt_total)
    other = arrived.reshape(nvirt, width, occ_block, occ_block, width)
    other = jnp.transpose(other, (3, 2, 1, 0, 4)).reshape(own.shape)

    partner = (index + npair // 2) % npair
    occ_i = lax.dynamic_slice_in_dim(occ_energy, index * occ_block, occ_block)
    occ_j = lax.dynamic_slice_in_dim(occ_energy, partner * occ_block, occ_block)
    virt_rows = lax.dynamic_slice_in_dim(virt_energy, place * width, width)
    denom = (
        occ_i[:, None, None, None]
        + occ_j[None, :, None, None]
        - virt_rows[None, None, :, None]
        - virt_energy[None, None, None, :]
    )
    updated = (
        block.astype(jnp.float32) + (own.astype(jnp.float32) + other.astype(jnp.float32)) / denom
    )
    return updated.astype(jnp.bfloat16)[None]


def solution(mesh):
    fine = Mesh(mesh.devices.reshape(X, ZL, C, ZH, Y), PAIR + VIRT)
    placed = (P(PAIR, None, None, VIRT, None), P(VIRT, PAIR), P(), P(), P())
    return jax.shard_map(
        local,
        mesh=fine,
        in_specs=placed,
        out_specs=P(PAIR, None, None, VIRT, None),
        check_vma=False,
    )
```

```python
import jax
import jax.numpy as jnp
from jax import lax
from jax.experimental import pallas as pl
from jax.experimental.pallas import tpu as pltpu
from jax.sharding import Mesh, PartitionSpec as P

X, ZL, C = 4, 4, 2
ZH, Y = 3, 8
PAIR = ("x", "zl", "c")
VIRT = ("zh", "y")
NVIRT = ZH * Y
BF16, F32 = jnp.bfloat16, jnp.float32
VMEM = pl.BlockSpec(memory_space=pltpu.VMEM)
SMEM = pl.BlockSpec(memory_space=pltpu.SMEM)
NT = (((1,), (1,)), ((), ()))


def passed_along(value, axis, steps):
    count = lax.axis_size(axis)
    pairs = [(source, (source + steps) % count) for source in range(count)]
    return lax.ppermute(value, axis, pairs)


def cycle_kernel(place, mine, theirs, t0, t1, t2a, t2b, t3, mirror, own0, own1, own2, own3):
    x, c = place[0], place[1]
    half = mine.shape[1]
    here = pl.ds(pl.multiple_of(c * half, 128), half)
    there = pl.ds(pl.multiple_of((1 - c) * half, 128), half)

    def product(t):
        total = lax.dot_general(mine[...], t[:, here], NT, preferred_element_type=F32)
        total += lax.dot_general(theirs[...], t[:, there], NT, preferred_element_type=F32)
        return total.astype(BF16)

    for steps, parts, own in ((0, (t0,), own0), (1, (t1,), own1), (2, (t2a, t2b), own2), (3, (t3,), own3)):
        slot = lax.rem(x + (X + X // 2 - steps), X)
        first = 0
        for part in parts:
            value = product(part)
            lanes = slice(first, first + part.shape[0])
            mirror[slot, :, lanes] = value
            own[:, lanes] = value
            first += part.shape[0]


def finish_kernel(place, arrived, own0, own1, own2, own3, t, row_term, virt, out, own_rows):
    x = place[0]
    quarter = arrived.shape[2]
    width = X * quarter
    lanes = arrived.shape[3]
    pieces = lanes // width
    for steps, own in enumerate((own0, own1, own2, own3)):
        slot = lax.rem(x + steps, X)
        own_rows[:, pl.ds(pl.multiple_of(slot * quarter, quarter), quarter), :] = own[...].reshape(
            NVIRT, quarter, lanes
        )
    rows = lax.broadcasted_iota(jnp.int32, (lanes, lanes), 0)
    columns = lax.broadcasted_iota(jnp.int32, (lanes, lanes), 1)
    unit = (rows == columns).astype(BF16)
    rows = lax.broadcasted_iota(jnp.int32, (2 * lanes, 2 * lanes), 0)
    columns = lax.broadcasted_iota(jnp.int32, (2 * lanes, 2 * lanes), 1)
    odd, rest = rows // lanes, rows % lanes
    target = (rest // width) * (2 * width) + odd * width + rest % width
    moved = (columns == target).astype(BF16)
    for group in range(NVIRT // 4):
        cut = slice(group * 4 * width, (group + 1) * 4 * width)
        own = lax.dot_general(
            unit,
            own_rows[4 * group : 4 * group + 4].reshape(4 * width, lanes),
            NT,
            preferred_element_type=F32,
        )
        sent = [arrived[:, 4 * group + k].reshape(width, lanes) for k in range(4)]
        stacked = jnp.concatenate(
            [
                jnp.concatenate([sent[0], sent[1]], axis=1),
                jnp.concatenate([sent[2], sent[3]], axis=1),
            ],
            axis=0,
        )
        spread = jnp.dot(stacked, moved, preferred_element_type=F32)
        for i in range(2):
            for j in range(2):
                at = slice((i * 2 + j) * width, (i * 2 + j + 1) * width)
                piece = slice((j * 2 + i) * 2 * width, (j * 2 + i + 1) * 2 * width)
                other = jnp.concatenate([spread[:width, piece], spread[width:, piece]], axis=1)
                denom = row_term[at, :] - virt[:, cut]
                change = (own[at, :] + other) / denom
                out[at, cut] = (t[at, cut].astype(F32) + change).astype(BF16)


def local(amplitudes, integrals, irreps, occ_energy, virt_energy):
    _, occ_block, _, width, virt_total = amplitudes.shape
    lanes = occ_block * occ_block * width
    flat = amplitudes.reshape(lanes, virt_total)
    depth = integrals.shape[1]
    quarter = width // X
    npair = X * ZL * C
    index = lax.axis_index(PAIR)
    place = lax.axis_index(VIRT)
    spot = jnp.stack([lax.axis_index("x"), lax.axis_index("c")]).astype(jnp.int32)

    t2a = passed_along(flat[: lanes // 2], "x", 2)
    t2b = passed_along(flat[lanes // 2 :], "x", 2)
    t1 = passed_along(flat, "x", 1)
    t3 = passed_along(flat, "x", 3)

    irreps_a = lax.dynamic_slice_in_dim(irreps, place * width, width)
    irreps_c = lax.dynamic_slice_in_dim(irreps, index * depth, depth)
    keep = irreps_a[:, None] == irreps_c[None, :]
    masked = jnp.where(keep, integrals, jnp.zeros_like(integrals))
    sent = jnp.broadcast_to(
        masked.reshape(X, 1, quarter, depth), (X, ZL * C, quarter, depth)
    ).reshape(npair, quarter, depth)
    rows = lax.all_to_all(sent, PAIR, split_axis=0, concat_axis=0, tiled=True)
    rows = jnp.transpose(rows, (1, 0, 2)).reshape(quarter, virt_total)
    rows = lax.dynamic_slice_in_dim(rows, lax.axis_index("c") * (virt_total // 2), virt_total // 2, axis=1)
    rows, t2a = lax.optimization_barrier((rows, t2a))
    copies = jnp.broadcast_to(rows[None], (NVIRT,) + rows.shape)
    mine = lax.all_to_all(copies, VIRT, split_axis=0, concat_axis=0, tiled=True)
    mine, t1, t3, t2b = lax.optimization_barrier((mine, t1, t3, t2b))
    mine = mine.reshape(NVIRT * quarter, virt_total // 2)
    theirs = passed_along(mine, "c", 1)

    share = jax.ShapeDtypeStruct((NVIRT * quarter, lanes), BF16)
    mirror, own0, own1, own2, own3 = pl.pallas_call(
        cycle_kernel,
        out_shape=[jax.ShapeDtypeStruct((X,) + share.shape, BF16)] + [share] * X,
        in_specs=[SMEM] + [VMEM] * 7,
        out_specs=[VMEM] * 5,
        cost_estimate=pl.CostEstimate(flops=1_210_000_000, bytes_accessed=6_000_000, transcendentals=0),
        compiler_params=pltpu.CompilerParams(vmem_limit_bytes=24 * 2**20),
        name="cycle",
    )(spot, mine, theirs, flat, t1, t2a, t2b, t3)

    arrived = lax.all_to_all(
        mirror.reshape(X * NVIRT, quarter, lanes), ("x",) + VIRT, split_axis=0, concat_axis=0, tiled=True
    ).reshape(X, NVIRT, quarter, lanes)
    own1 = passed_along(own1, "x", -1)
    own2 = passed_along(own2, "x", -2)
    own3 = passed_along(own3, "x", -3)

    partner = (index + npair // 2) % npair
    occ_i = lax.dynamic_slice_in_dim(occ_energy, index * occ_block, occ_block)
    occ_j = lax.dynamic_slice_in_dim(occ_energy, partner * occ_block, occ_block)
    virt_rows = lax.dynamic_slice_in_dim(virt_energy, place * width, width)
    row_term = (occ_i[:, None, None] + occ_j[None, :, None] - virt_rows[None, None, :]).reshape(lanes, 1)
    updated = pl.pallas_call(
        finish_kernel,
        out_shape=jax.ShapeDtypeStruct(flat.shape, BF16),
        in_specs=[SMEM] + [VMEM] * 8,
        out_specs=VMEM,
        scratch_shapes=[pltpu.VMEM((NVIRT, width, lanes), BF16)],
        cost_estimate=pl.CostEstimate(flops=600_000_000, bytes_accessed=4_000_000, transcendentals=0),
        compiler_params=pltpu.CompilerParams(vmem_limit_bytes=24 * 2**20),
        name="finish",
    )(spot, arrived, own0, own1, own2, own3, flat, row_term, virt_energy[None, :])
    return updated.reshape(amplitudes.shape)


def solution(mesh):
    fine = Mesh(mesh.devices.reshape(X, ZL, C, ZH, Y), PAIR + VIRT)
    placed = (P(PAIR, None, None, VIRT, None), P(VIRT, PAIR), P(), P(), P())
    return jax.shard_map(
        local,
        mesh=fine,
        in_specs=placed,
        out_specs=P(PAIR, None, None, VIRT, None),
        check_vma=False,
    )
```

```python
import jax
import jax.numpy as jnp
from jax import lax
from jax.experimental import pallas as pl
from jax.experimental.pallas import tpu as pltpu
from jax.sharding import Mesh, PartitionSpec as P

X, ZL, C = 4, 4, 2
ZH, Y = 3, 8
PAIR = ("x", "zl", "c")
VIRT = ("zh", "y")
NVIRT = ZH * Y
BF16, F32 = jnp.bfloat16, jnp.float32
VMEM = pl.BlockSpec(memory_space=pltpu.VMEM)
SMEM = pl.BlockSpec(memory_space=pltpu.SMEM)
NT = (((1,), (1,)), ((), ()))


def passed_along(value, axis, steps):
    count = lax.axis_size(axis)
    pairs = [(source, (source + steps) % count) for source in range(count)]
    return lax.ppermute(value, axis, pairs)


def cycle_kernel(place, mine, theirs, t0, t1, t2a, t2b, t3, mirror, own0, own1, own2, own3):
    x, c = place[0], place[1]
    half = mine.shape[1]
    quarter = mirror.shape[1] // X
    here = pl.ds(pl.multiple_of(c * half, 128), half)
    there = pl.ds(pl.multiple_of((1 - c) * half, 128), half)

    def product(t):
        total = lax.dot_general(mine[...], t[:, here], NT, preferred_element_type=F32)
        total += lax.dot_general(theirs[...], t[:, there], NT, preferred_element_type=F32)
        return total.astype(BF16)

    for steps, parts, own in ((0, (t0,), own0), (1, (t1,), own1), (2, (t2a, t2b), own2), (3, (t3,), own3)):
        slot = lax.rem(x + (X + X // 2 - steps), X)
        first = 0
        for part in parts:
            value = product(part)
            lanes = slice(first, first + part.shape[0])
            mirror[:, pl.ds(pl.multiple_of(slot * quarter, quarter), quarter), lanes] = value.reshape(
                NVIRT, quarter, part.shape[0]
            )
            own[:, lanes] = value
            first += part.shape[0]


def finish_kernel(place, arrived, own0, own1, own2, own3, t, row_term, virt, out, own_rows):
    x = place[0]
    width, lanes = arrived.shape[1:]
    quarter = width // X
    pieces = lanes // width
    for steps, own in enumerate((own0, own1, own2, own3)):
        slot = lax.rem(x + steps, X)
        own_rows[:, pl.ds(pl.multiple_of(slot * quarter, quarter), quarter), :] = own[...].reshape(
            NVIRT, quarter, lanes
        )
    rows = lax.broadcasted_iota(jnp.int32, (lanes, lanes), 0)
    columns = lax.broadcasted_iota(jnp.int32, (lanes, lanes), 1)
    unit = (rows == columns).astype(BF16)
    rows = lax.broadcasted_iota(jnp.int32, (2 * lanes, 2 * lanes), 0)
    columns = lax.broadcasted_iota(jnp.int32, (2 * lanes, 2 * lanes), 1)
    odd, rest = rows // lanes, rows % lanes
    target = (rest // width) * (2 * width) + odd * width + rest % width
    moved = (columns == target).astype(BF16)
    for group in range(NVIRT // 4):
        cut = slice(group * 4 * width, (group + 1) * 4 * width)
        own = lax.dot_general(
            unit,
            own_rows[4 * group : 4 * group + 4].reshape(4 * width, lanes),
            NT,
            preferred_element_type=F32,
        )
        sent = [arrived[4 * group + k] for k in range(4)]
        stacked = jnp.concatenate(
            [
                jnp.concatenate([sent[0], sent[1]], axis=1),
                jnp.concatenate([sent[2], sent[3]], axis=1),
            ],
            axis=0,
        )
        spread = jnp.dot(stacked, moved, preferred_element_type=F32)
        for i in range(2):
            for j in range(2):
                at = slice((i * 2 + j) * width, (i * 2 + j + 1) * width)
                piece = slice((j * 2 + i) * 2 * width, (j * 2 + i + 1) * 2 * width)
                other = jnp.concatenate([spread[:width, piece], spread[width:, piece]], axis=1)
                denom = row_term[at, :] - virt[:, cut]
                change = (own[at, :] + other) / denom
                out[at, cut] = (t[at, cut].astype(F32) + change).astype(BF16)


def local(amplitudes, integrals, irreps, occ_energy, virt_energy):
    _, occ_block, _, width, virt_total = amplitudes.shape
    lanes = occ_block * occ_block * width
    flat = amplitudes.reshape(lanes, virt_total)
    depth = integrals.shape[1]
    quarter = width // X
    npair = X * ZL * C
    index = lax.axis_index(PAIR)
    place = lax.axis_index(VIRT)
    spot = jnp.stack([lax.axis_index("x"), lax.axis_index("c")]).astype(jnp.int32)

    t1 = passed_along(flat, "x", 1)
    t3 = passed_along(flat, "x", 3)

    irreps_a = lax.dynamic_slice_in_dim(irreps, place * width, width)
    irreps_c = lax.dynamic_slice_in_dim(irreps, index * depth, depth)
    keep = irreps_a[:, None] == irreps_c[None, :]
    masked = jnp.where(keep, integrals, jnp.zeros_like(integrals))
    sent = jnp.broadcast_to(
        masked.reshape(X, 1, quarter, depth), (X, ZL * C, quarter, depth)
    ).reshape(npair, quarter, depth)
    rows = lax.all_to_all(sent, PAIR, split_axis=0, concat_axis=0, tiled=True)
    rows = jnp.transpose(rows, (1, 0, 2)).reshape(quarter, virt_total)
    rows = lax.dynamic_slice_in_dim(rows, lax.axis_index("c") * (virt_total // 2), virt_total // 2, axis=1)
    rows, t1, t3 = lax.optimization_barrier((rows, t1, t3))
    t2a = passed_along(t1[: lanes // 2], "x", 1)
    t2b = passed_along(t3[lanes // 2 :], "x", 3)
    copies = jnp.broadcast_to(rows[None], (NVIRT,) + rows.shape)
    mine = lax.all_to_all(copies, VIRT, split_axis=0, concat_axis=0, tiled=True)
    mine, t2a, t2b = lax.optimization_barrier((mine, t2a, t2b))
    mine = mine.reshape(NVIRT * quarter, virt_total // 2)
    theirs = passed_along(mine, "c", 1)

    share = jax.ShapeDtypeStruct((NVIRT * quarter, lanes), BF16)
    mirror, own0, own1, own2, own3 = pl.pallas_call(
        cycle_kernel,
        out_shape=[jax.ShapeDtypeStruct((NVIRT, width, lanes), BF16)] + [share] * X,
        in_specs=[SMEM] + [VMEM] * 7,
        out_specs=[VMEM] * 5,
        cost_estimate=pl.CostEstimate(flops=1_210_000_000, bytes_accessed=6_000_000, transcendentals=0),
        compiler_params=pltpu.CompilerParams(vmem_limit_bytes=12 * 2**20),
        name="cycle",
    )(spot, mine, theirs, flat, t1, t2a, t2b, t3)

    arrived = lax.all_to_all(
        mirror.reshape(NVIRT * X, quarter, lanes), VIRT + ("x",), split_axis=0, concat_axis=0, tiled=True
    ).reshape(NVIRT, width, lanes)
    own1 = passed_along(own1, "x", -1)
    own2 = passed_along(own2, "x", -2)
    own3 = passed_along(own3, "x", -3)

    partner = (index + npair // 2) % npair
    occ_i = lax.dynamic_slice_in_dim(occ_energy, index * occ_block, occ_block)
    occ_j = lax.dynamic_slice_in_dim(occ_energy, partner * occ_block, occ_block)
    virt_rows = lax.dynamic_slice_in_dim(virt_energy, place * width, width)
    row_term = (occ_i[:, None, None] + occ_j[None, :, None] - virt_rows[None, None, :]).reshape(lanes, 1)
    updated = pl.pallas_call(
        finish_kernel,
        out_shape=jax.ShapeDtypeStruct(flat.shape, BF16),
        in_specs=[SMEM] + [VMEM] * 8,
        out_specs=VMEM,
        scratch_shapes=[pltpu.VMEM((NVIRT, width, lanes), BF16)],
        cost_estimate=pl.CostEstimate(flops=600_000_000, bytes_accessed=4_000_000, transcendentals=0),
        compiler_params=pltpu.CompilerParams(vmem_limit_bytes=12 * 2**20),
        name="finish",
    )(spot, arrived, own0, own1, own2, own3, flat, row_term, virt_energy[None, :])
    return updated.reshape(amplitudes.shape)


def solution(mesh):
    fine = Mesh(mesh.devices.reshape(X, ZL, C, ZH, Y), PAIR + VIRT)
    placed = (P(PAIR, None, None, VIRT, None), P(VIRT, PAIR), P(), P(), P())
    return jax.shard_map(
        local,
        mesh=fine,
        in_specs=placed,
        out_specs=P(PAIR, None, None, VIRT, None),
        check_vma=False,
    )
```

```python
import functools

import jax
import jax.numpy as jnp
from jax import lax
from jax.experimental import pallas as pl
from jax.experimental.pallas import tpu as pltpu
from jax.sharding import Mesh, PartitionSpec as P

X, ZL, C = 4, 4, 2
ZH, Y = 3, 8
PAIR = ("x", "zl", "c")
VIRT = ("zh", "y")
NVIRT = ZH * Y
BF16, F32 = jnp.bfloat16, jnp.float32
VMEM = pl.BlockSpec(memory_space=pltpu.VMEM)
SMEM = pl.BlockSpec(memory_space=pltpu.SMEM)
HBM = pl.BlockSpec(memory_space=pltpu.HBM)
NT = (((1,), (1,)), ((), ()))


def passed_along(value, axis, steps):
    count = lax.axis_size(axis)
    pairs = [(source, (source + steps) % count) for source in range(count)]
    return lax.ppermute(value, axis, pairs)


def mask_kernel(place, irreps, rows, out):
    total = irreps.shape[1]
    lanes = rows.shape[1]
    quarter = out.shape[1]
    copies = out.shape[0] // X
    labels = jnp.broadcast_to(irreps[...], (8, total))
    of_row = pltpu.roll(labels, lax.rem(total - place[2], total), 1)[:1, :lanes].astype(F32)
    of_column = pltpu.roll(labels, lax.rem(total - place[3], total), 1)[:1, :lanes].astype(F32)
    of_row = jnp.transpose(jnp.broadcast_to(of_row, (lanes, lanes)))[: rows.shape[0]]
    masked = jnp.where(of_row == of_column, rows[...].astype(F32), 0.0).astype(BF16)
    for share in range(X):
        piece = masked[share * quarter : (share + 1) * quarter]
        for copy in range(copies):
            out[share * copies + copy] = piece


def gather_kernel(place, pieces, out, depth):
    c = place[1]
    quarter = pieces.shape[1]
    count = pieces.shape[0] // 2
    lane = lax.broadcasted_iota(jnp.int32, (quarter, 128), 1)
    tiles = [jnp.zeros((quarter, 128), F32) for _ in range(out.shape[2] // 128)]
    for number in range(count):
        tile, start = divmod(number * depth, 128)
        piece = pltpu.roll(pieces[c * count + number].astype(F32), start, 1)
        if start + depth <= 128:
            tiles[tile] += piece
        else:
            tiles[tile] += jnp.where(lane >= start, piece, 0.0)
            tiles[tile + 1] += jnp.where(lane < start, piece, 0.0)
    half = jnp.concatenate(tiles, axis=1).astype(BF16)
    for copy in range(NVIRT):
        out[copy] = half


def cycle_kernel(
    place, mine, theirs, t0, t1, t2a, t2b, t3, mirror, own0, own1, own2, own3, held, done, in_sems, out_sems
):
    x, c = place[0], place[1]
    half = mine.shape[1]
    quarter = mirror.shape[1] // X
    rows = t2a.shape[0]
    here = pl.ds(pl.multiple_of(c * half, 128), half)
    there = pl.ds(pl.multiple_of((1 - c) * half, 128), half)
    loads = [
        pltpu.make_async_copy(source, target, in_sems.at[number])
        for number, (source, target) in enumerate(
            (
                (t0, held.at[0]),
                (t1, held.at[1]),
                (t3, held.at[3]),
                (t2a, held.at[2, pl.ds(0, rows)]),
                (t2b, held.at[2, pl.ds(rows, rows)]),
            )
        )
    ]
    for load in loads:
        load.start()
    stores = []
    for steps, needed, own in (
        (0, loads[:1], own0),
        (1, loads[1:2], own1),
        (3, loads[2:3], own3),
        (2, loads[3:], own2),
    ):
        for load in needed:
            load.wait()
        total = lax.dot_general(mine[...], held[steps, :, here], NT, preferred_element_type=F32)
        total += lax.dot_general(theirs[...], held[steps, :, there], NT, preferred_element_type=F32)
        slot = lax.rem(x + (X + X // 2 - steps), X)
        done[steps] = total.astype(BF16).reshape(done.shape[1:])
        target = mirror.at[:, pl.ds(pl.multiple_of(slot * quarter, quarter), quarter), :]
        for which, place_of in enumerate((own, target)):
            store = pltpu.make_async_copy(done.at[steps], place_of, out_sems.at[steps, which])
            store.start()
            stores.append(store)
    for store in stores:
        store.wait()


def finish_kernel(place, arrived, own0, own1, own2, own3, t, row_term, virt, out, own_rows):
    x = place[0]
    width, lanes = arrived.shape[1:]
    quarter = width // X
    pieces = lanes // width
    for steps, own in enumerate((own0, own1, own2, own3)):
        slot = lax.rem(x + steps, X)
        own_rows[:, pl.ds(pl.multiple_of(slot * quarter, quarter), quarter), :] = own[...]
    rows = lax.broadcasted_iota(jnp.int32, (lanes, lanes), 0)
    columns = lax.broadcasted_iota(jnp.int32, (lanes, lanes), 1)
    unit = (rows == columns).astype(BF16)
    rows = lax.broadcasted_iota(jnp.int32, (2 * lanes, 2 * lanes), 0)
    columns = lax.broadcasted_iota(jnp.int32, (2 * lanes, 2 * lanes), 1)
    odd, rest = rows // lanes, rows % lanes
    target = (rest // width) * (2 * width) + odd * width + rest % width
    moved = (columns == target).astype(BF16)
    for group in range(NVIRT // 4):
        cut = slice(group * 4 * width, (group + 1) * 4 * width)
        own = lax.dot_general(
            unit,
            own_rows[4 * group : 4 * group + 4].reshape(4 * width, lanes),
            NT,
            preferred_element_type=F32,
        )
        sent = [arrived[4 * group + k] for k in range(4)]
        stacked = jnp.concatenate(
            [
                jnp.concatenate([sent[0], sent[1]], axis=1),
                jnp.concatenate([sent[2], sent[3]], axis=1),
            ],
            axis=0,
        )
        spread = jnp.dot(stacked, moved, preferred_element_type=F32)
        for i in range(2):
            for j in range(2):
                at = slice((i * 2 + j) * width, (i * 2 + j + 1) * width)
                piece = slice((j * 2 + i) * 2 * width, (j * 2 + i + 1) * 2 * width)
                other = jnp.concatenate([spread[:width, piece], spread[width:, piece]], axis=1)
                denom = row_term[at, :] - virt[:, cut]
                change = (own[at, :] + other) / denom
                out[at, cut] = (t[at, cut].astype(F32) + change).astype(BF16)


def local(amplitudes, integrals, irreps, occ_energy, virt_energy):
    _, occ_block, _, width, virt_total = amplitudes.shape
    lanes = occ_block * occ_block * width
    flat = amplitudes.reshape(lanes, virt_total)
    depth = integrals.shape[1]
    quarter = width // X
    npair = X * ZL * C
    index = lax.axis_index(PAIR)
    place = lax.axis_index(VIRT)
    spot = jnp.stack(
        [lax.axis_index("x"), lax.axis_index("c"), place * width, index * depth]
    ).astype(jnp.int32)

    t1 = passed_along(flat, "x", 1)
    t3 = passed_along(flat, "x", 3)

    sent = pl.pallas_call(
        mask_kernel,
        out_shape=jax.ShapeDtypeStruct((npair, quarter, 128), BF16),
        in_specs=[SMEM, VMEM, VMEM],
        out_specs=VMEM,
        cost_estimate=pl.CostEstimate(flops=100_000, bytes_accessed=150_000, transcendentals=0),
        name="mask",
    )(spot, irreps[None, :], jnp.pad(integrals, ((0, 0), (0, 128 - depth))))
    pieces = lax.all_to_all(sent, PAIR, split_axis=0, concat_axis=0, tiled=True)
    pieces, t1, t3 = lax.optimization_barrier((pieces, t1, t3))
    copies = pl.pallas_call(
        functools.partial(gather_kernel, depth=depth),
        out_shape=jax.ShapeDtypeStruct((NVIRT, quarter, virt_total // 2), BF16),
        in_specs=[SMEM, VMEM],
        out_specs=VMEM,
        cost_estimate=pl.CostEstimate(flops=100_000, bytes_accessed=700_000, transcendentals=0),
        name="gather",
    )(spot, pieces)
    t2a = passed_along(t1[: lanes // 2], "x", 1)
    t2b = passed_along(t3[lanes // 2 :], "x", 3)
    mine = lax.all_to_all(copies, VIRT, split_axis=0, concat_axis=0, tiled=True)
    mine, t2a, t2b = lax.optimization_barrier((mine, t2a, t2b))
    mine = mine.reshape(NVIRT * quarter, virt_total // 2)
    theirs = passed_along(mine, "c", 1)

    share = jax.ShapeDtypeStruct((NVIRT, quarter, lanes), BF16)
    mirror, own0, own1, own2, own3 = pl.pallas_call(
        cycle_kernel,
        out_shape=[jax.ShapeDtypeStruct((NVIRT, width, lanes), BF16)] + [share] * X,
        in_specs=[SMEM] + [VMEM] * 2 + [HBM] * 5,
        out_specs=[HBM] * 5,
        scratch_shapes=[
            pltpu.VMEM((X, lanes, virt_total), BF16),
            pltpu.VMEM((X,) + share.shape, BF16),
            pltpu.SemaphoreType.DMA((5,)),
            pltpu.SemaphoreType.DMA((X, 2)),
        ],
        cost_estimate=pl.CostEstimate(flops=1_210_000_000, bytes_accessed=6_000_000, transcendentals=0),
        compiler_params=pltpu.CompilerParams(vmem_limit_bytes=12 * 2**20),
        name="cycle",
    )(spot, mine, theirs, flat, t1, t2a, t2b, t3)

    arrived = lax.all_to_all(
        mirror.reshape(NVIRT * X, quarter, lanes), VIRT + ("x",), split_axis=0, concat_axis=0, tiled=True
    ).reshape(NVIRT, width, lanes)
    own1 = passed_along(own1, "x", -1)
    own2 = passed_along(own2, "x", -2)
    own3 = passed_along(own3, "x", -3)

    partner = (index + npair // 2) % npair
    occ_i = lax.dynamic_slice_in_dim(occ_energy, index * occ_block, occ_block)
    occ_j = lax.dynamic_slice_in_dim(occ_energy, partner * occ_block, occ_block)
    virt_rows = lax.dynamic_slice_in_dim(virt_energy, place * width, width)
    row_term = (occ_i[:, None, None] + occ_j[None, :, None] - virt_rows[None, None, :]).reshape(lanes, 1)
    updated = pl.pallas_call(
        finish_kernel,
        out_shape=jax.ShapeDtypeStruct(flat.shape, BF16),
        in_specs=[SMEM] + [VMEM] * 8,
        out_specs=VMEM,
        scratch_shapes=[pltpu.VMEM((NVIRT, width, lanes), BF16)],
        cost_estimate=pl.CostEstimate(flops=600_000_000, bytes_accessed=4_000_000, transcendentals=0),
        compiler_params=pltpu.CompilerParams(vmem_limit_bytes=12 * 2**20),
        name="finish",
    )(spot, arrived, own0, own1, own2, own3, flat, row_term, virt_energy[None, :])
    return updated.reshape(amplitudes.shape)


def solution(mesh):
    fine = Mesh(mesh.devices.reshape(X, ZL, C, ZH, Y), PAIR + VIRT)
    placed = (P(PAIR, None, None, VIRT, None), P(VIRT, PAIR), P(), P(), P())
    return jax.shard_map(
        local,
        mesh=fine,
        in_specs=placed,
        out_specs=P(PAIR, None, None, VIRT, None),
        check_vma=False,
    )
```

```python
import jax
import jax.numpy as jnp
from jax import lax
from jax.experimental import pallas as pl
from jax.experimental.pallas import tpu as pltpu
from jax.sharding import Mesh, PartitionSpec as P

X, ZL, C = 4, 4, 2
ZH, Y = 3, 8
PAIR = ("x", "zl", "c")
VIRT = ("zh", "y")
NVIRT = ZH * Y
BF16, F32 = jnp.bfloat16, jnp.float32
VMEM = pl.BlockSpec(memory_space=pltpu.VMEM)
SMEM = pl.BlockSpec(memory_space=pltpu.SMEM)
NT = (((1,), (1,)), ((), ()))


def passed_along(value, axis, steps):
    count = lax.axis_size(axis)
    pairs = [(source, (source + steps) % count) for source in range(count)]
    return lax.ppermute(value, axis, pairs)


def unit_matrix(size):
    rows = lax.broadcasted_iota(jnp.int32, (size, size), 0)
    return (rows == lax.broadcasted_iota(jnp.int32, (size, size), 1)).astype(BF16)


def spread(value, axis, count):
    copies = jnp.broadcast_to(value[None], (count,) + value.shape)
    return lax.all_to_all(copies, axis, split_axis=0, concat_axis=0, tiled=True)


def turn_kernel(labels_c, labels_a, pieces, out):
    depth = pieces.shape[2]
    quarter = pieces.shape[1] // X
    unit = unit_matrix(depth)
    for share in range(X):
        rows = pieces[:, share * quarter : (share + 1) * quarter, :].reshape(NVIRT * quarter, depth)
        turned = lax.dot_general(unit, rows, NT, preferred_element_type=F32)
        keep = labels_c[...] == labels_a[share : share + 1, :]
        masked = jnp.where(keep, turned, 0.0).astype(BF16)
        for copy in range(ZL):
            out[share * ZL + copy] = masked


def cycle_kernel(
    place, mine, theirs, t0, t1, t2a, t2b, t2c, t2d, t3, mirror, own0, own1, own2, own3, turned, held, t2
):
    x, c = place[0], place[1]
    quarter = mirror.shape[1] // X
    count, depth, size = mine.shape
    for number in range(count):
        here = pl.multiple_of((2 * number + c) * depth, 16)
        there = pl.multiple_of((2 * number + 1 - c) * depth, 16)
        turned[pl.ds(here, depth), :] = mine[number]
        turned[pl.ds(there, depth), :] = theirs[number]
    unit = unit_matrix(size)
    for first in range(0, turned.shape[0], size):
        part = lax.dot_general(unit, turned[first : first + size, :], NT, preferred_element_type=F32)
        held[:, first : first + size] = part.astype(BF16)
    rows = t2a.shape[0]
    for number, part in enumerate((t2a, t2b, t2c, t2d)):
        t2[number * rows : (number + 1) * rows, :] = part[...]
    for steps, (t, own) in enumerate(((t0, own0), (t1, own1), (t2, own2), (t3, own3))):
        slot = lax.rem(x + (X + X // 2 - steps), X)
        value = lax.dot_general(held[...], t[...], NT, preferred_element_type=F32).astype(BF16)
        mirror[:, pl.ds(pl.multiple_of(slot * quarter, quarter), quarter), :] = value.reshape(
            NVIRT, quarter, value.shape[1]
        )
        own[...] = value


def finish_kernel(place, arrived, own0, own1, own2, own3, t, row_term, virt, out, own_rows):
    x = place[0]
    width, lanes = arrived.shape[1:]
    quarter = width // X
    pieces = lanes // width
    for steps, own in enumerate((own0, own1, own2, own3)):
        slot = lax.rem(x + steps, X)
        own_rows[:, pl.ds(pl.multiple_of(slot * quarter, quarter), quarter), :] = own[...].reshape(
            NVIRT, quarter, lanes
        )
    rows = lax.broadcasted_iota(jnp.int32, (lanes, lanes), 0)
    columns = lax.broadcasted_iota(jnp.int32, (lanes, lanes), 1)
    unit = (rows == columns).astype(BF16)
    rows = lax.broadcasted_iota(jnp.int32, (2 * lanes, 2 * lanes), 0)
    columns = lax.broadcasted_iota(jnp.int32, (2 * lanes, 2 * lanes), 1)
    odd, rest = rows // lanes, rows % lanes
    target = (rest // width) * (2 * width) + odd * width + rest % width
    moved = (columns == target).astype(BF16)
    for group in range(NVIRT // 4):
        cut = slice(group * 4 * width, (group + 1) * 4 * width)
        own = lax.dot_general(
            unit,
            own_rows[4 * group : 4 * group + 4].reshape(4 * width, lanes),
            NT,
            preferred_element_type=F32,
        )
        sent = [arrived[4 * group + k] for k in range(4)]
        stacked = jnp.concatenate(
            [
                jnp.concatenate([sent[0], sent[1]], axis=1),
                jnp.concatenate([sent[2], sent[3]], axis=1),
            ],
            axis=0,
        )
        spread = jnp.dot(stacked, moved, preferred_element_type=F32)
        for i in range(2):
            for j in range(2):
                at = slice((i * 2 + j) * width, (i * 2 + j + 1) * width)
                piece = slice((j * 2 + i) * 2 * width, (j * 2 + i + 1) * 2 * width)
                other = jnp.concatenate([spread[:width, piece], spread[width:, piece]], axis=1)
                denom = row_term[at, :] - virt[:, cut]
                change = (own[at, :] + other) / denom
                out[at, cut] = (t[at, cut].astype(F32) + change).astype(BF16)


def local(amplitudes, integrals, irreps, occ_energy, virt_energy):
    _, occ_block, _, width, virt_total = amplitudes.shape
    lanes = occ_block * occ_block * width
    flat = amplitudes.reshape(lanes, virt_total)
    depth = integrals.shape[1]
    quarter = width // X
    npair = X * ZL * C
    index = lax.axis_index(PAIR)
    place = lax.axis_index(VIRT)
    spot = jnp.stack([lax.axis_index("x"), lax.axis_index("c")]).astype(jnp.int32)

    t1 = passed_along(flat, "x", 1)
    t3 = passed_along(flat, "x", 3)

    pieces = spread(integrals, VIRT, NVIRT)
    labels_c = lax.dynamic_slice_in_dim(irreps, index * depth, depth)[:, None]
    labels_a = jnp.transpose(irreps.reshape(NVIRT, X, quarter), (1, 0, 2)).reshape(X, NVIRT * quarter)
    part = lanes // 4
    t2a = passed_along(t1[:part], "x", 1)
    t2d = passed_along(t3[3 * part :], "x", 3)
    pieces, t1, t3, t2a, t2d = lax.optimization_barrier((pieces, t1, t3, t2a, t2d))
    t2b = passed_along(t1[part : 2 * part], "x", 1)
    t2c = passed_along(t3[2 * part : 3 * part], "x", 3)
    sent = pl.pallas_call(
        turn_kernel,
        out_shape=jax.ShapeDtypeStruct((X * ZL, depth, NVIRT * quarter), BF16),
        in_specs=[VMEM] * 3,
        out_specs=VMEM,
        cost_estimate=pl.CostEstimate(flops=10_000_000, bytes_accessed=1_000_000, transcendentals=0),
        compiler_params=pltpu.CompilerParams(vmem_limit_bytes=12 * 2**20),
        name="turn",
    )(labels_c, labels_a, pieces)
    mine = lax.all_to_all(sent, ("x", "zl"), split_axis=0, concat_axis=0, tiled=True)
    mine, t2b, t2c = lax.optimization_barrier((mine, t2b, t2c))
    theirs = passed_along(mine, "c", 1)

    share = jax.ShapeDtypeStruct((NVIRT * quarter, lanes), BF16)
    mirror, own0, own1, own2, own3 = pl.pallas_call(
        cycle_kernel,
        out_shape=[jax.ShapeDtypeStruct((NVIRT, width, lanes), BF16)] + [share] * X,
        in_specs=[SMEM] + [VMEM] * 9,
        out_specs=[VMEM] * 5,
        scratch_shapes=[
            pltpu.VMEM((virt_total, NVIRT * quarter), BF16),
            pltpu.VMEM((NVIRT * quarter, virt_total), BF16),
            pltpu.VMEM(flat.shape, BF16),
        ],
        cost_estimate=pl.CostEstimate(flops=1_210_000_000, bytes_accessed=6_000_000, transcendentals=0),
        compiler_params=pltpu.CompilerParams(vmem_limit_bytes=56 * 2**20),
        name="cycle",
    )(spot, mine, theirs, flat, t1, t2a, t2b, t2c, t2d, t3)

    arrived = lax.all_to_all(
        mirror.reshape(NVIRT * X, quarter, lanes), VIRT + ("x",), split_axis=0, concat_axis=0, tiled=True
    ).reshape(NVIRT, width, lanes)
    own1 = passed_along(own1, "x", -1)
    own2 = passed_along(own2, "x", -2)
    own3 = passed_along(own3, "x", -3)

    partner = (index + npair // 2) % npair
    occ_i = lax.dynamic_slice_in_dim(occ_energy, index * occ_block, occ_block)
    occ_j = lax.dynamic_slice_in_dim(occ_energy, partner * occ_block, occ_block)
    virt_rows = lax.dynamic_slice_in_dim(virt_energy, place * width, width)
    row_term = (occ_i[:, None, None] + occ_j[None, :, None] - virt_rows[None, None, :]).reshape(lanes, 1)
    updated = pl.pallas_call(
        finish_kernel,
        out_shape=jax.ShapeDtypeStruct(flat.shape, BF16),
        in_specs=[SMEM] + [VMEM] * 8,
        out_specs=VMEM,
        scratch_shapes=[pltpu.VMEM((NVIRT, width, lanes), BF16)],
        cost_estimate=pl.CostEstimate(flops=600_000_000, bytes_accessed=4_000_000, transcendentals=0),
        compiler_params=pltpu.CompilerParams(vmem_limit_bytes=12 * 2**20),
        name="finish",
    )(spot, arrived, own0, own1, own2, own3, flat, row_term, virt_energy[None, :])
    return updated.reshape(amplitudes.shape)


def solution(mesh):
    fine = Mesh(mesh.devices.reshape(X, ZL, C, ZH, Y), PAIR + VIRT)
    placed = (P(PAIR, None, None, VIRT, None), P(VIRT, PAIR), P(), P(), P())
    return jax.shard_map(
        local,
        mesh=fine,
        in_specs=placed,
        out_specs=P(PAIR, None, None, VIRT, None),
        check_vma=False,
    )
```

```python
import jax
import jax.numpy as jnp
from jax import lax
from jax.experimental import pallas as pl
from jax.experimental.pallas import tpu as pltpu
from jax.sharding import Mesh, PartitionSpec as P

X, ZL, C = 4, 4, 2
ZH, Y = 3, 8
PAIR = ("x", "zl", "c")
VIRT = ("zh", "y")
NVIRT = ZH * Y
BF16, F32 = jnp.bfloat16, jnp.float32
VMEM = pl.BlockSpec(memory_space=pltpu.VMEM)
NT = (((1,), (1,)), ((), ()))


def passed_along(value, axis, steps):
    count = lax.axis_size(axis)
    pairs = [(source, (source + steps) % count) for source in range(count)]
    return lax.ppermute(value, axis, pairs)


def unit_matrix(size):
    rows = lax.broadcasted_iota(jnp.int32, (size, size), 0)
    return (rows == lax.broadcasted_iota(jnp.int32, (size, size), 1)).astype(BF16)


def spread(value, axis, count):
    copies = jnp.broadcast_to(value[None], (count,) + value.shape)
    return lax.all_to_all(copies, axis, split_axis=0, concat_axis=0, tiled=True)


def turn_kernel(labels_c, labels_a, pieces, out):
    depth = pieces.shape[2]
    quarter = pieces.shape[1] // X
    unit = unit_matrix(depth)
    for share in range(X):
        rows = pieces[:, share * quarter : (share + 1) * quarter, :].reshape(NVIRT * quarter, depth)
        turned = lax.dot_general(unit, rows, NT, preferred_element_type=F32)
        keep = labels_c[...] == labels_a[share : share + 1, :]
        masked = jnp.where(keep, turned, 0.0).astype(BF16)
        for copy in range(ZL):
            out[share * ZL + copy] = masked


def cycle_kernel(
    mine, theirs, t0, t1, t2a, t2b, t2c, t3, mirror, own0, own1, own2, own3, turned, held, t2
):
    x, c = lax.axis_index("x"), lax.axis_index("c")
    quarter = mirror.shape[1] // X
    count, depth, size = mine.shape
    for number in range(count):
        here = pl.multiple_of((2 * number + c) * depth, 16)
        there = pl.multiple_of((2 * number + 1 - c) * depth, 16)
        turned[pl.ds(here, depth), :] = mine[number]
        turned[pl.ds(there, depth), :] = theirs[number]
    unit = unit_matrix(size)
    for first in range(0, turned.shape[0], size):
        part = lax.dot_general(unit, turned[first : first + size, :], NT, preferred_element_type=F32)
        held[:, first : first + size] = part.astype(BF16)
    first = 0
    for part in (t2a, t2b, t2c):
        t2[first : first + part.shape[0], :] = part[...]
        first += part.shape[0]
    for steps, (t, own) in enumerate(((t0, own0), (t1, own1), (t2, own2), (t3, own3))):
        slot = lax.rem(x + (X + X // 2 - steps), X)
        value = lax.dot_general(held[...], t[...], NT, preferred_element_type=F32).astype(BF16)
        mirror[:, pl.ds(pl.multiple_of(slot * quarter, quarter), quarter), :] = value.reshape(
            NVIRT, quarter, value.shape[1]
        )
        own[...] = value


def finish_kernel(arrived, own0, own1, own2, own3, t, row_term, virt, out, own_rows):
    x = lax.axis_index("x")
    width, lanes = arrived.shape[1:]
    quarter = width // X
    pieces = lanes // width
    for steps, own in enumerate((own0, own1, own2, own3)):
        slot = lax.rem(x + steps, X)
        own_rows[:, pl.ds(pl.multiple_of(slot * quarter, quarter), quarter), :] = own[...].reshape(
            NVIRT, quarter, lanes
        )
    rows = lax.broadcasted_iota(jnp.int32, (lanes, lanes), 0)
    columns = lax.broadcasted_iota(jnp.int32, (lanes, lanes), 1)
    unit = (rows == columns).astype(BF16)
    rows = lax.broadcasted_iota(jnp.int32, (2 * lanes, 2 * lanes), 0)
    columns = lax.broadcasted_iota(jnp.int32, (2 * lanes, 2 * lanes), 1)
    odd, rest = rows // lanes, rows % lanes
    target = (rest // width) * (2 * width) + odd * width + rest % width
    moved = (columns == target).astype(BF16)
    for group in range(NVIRT // 4):
        cut = slice(group * 4 * width, (group + 1) * 4 * width)
        own = lax.dot_general(
            unit,
            own_rows[4 * group : 4 * group + 4].reshape(4 * width, lanes),
            NT,
            preferred_element_type=F32,
        )
        sent = [arrived[4 * group + k] for k in range(4)]
        stacked = jnp.concatenate(
            [
                jnp.concatenate([sent[0], sent[1]], axis=1),
                jnp.concatenate([sent[2], sent[3]], axis=1),
            ],
            axis=0,
        )
        spread = jnp.dot(stacked, moved, preferred_element_type=F32)
        for i in range(2):
            for j in range(2):
                at = slice((i * 2 + j) * width, (i * 2 + j + 1) * width)
                piece = slice((j * 2 + i) * 2 * width, (j * 2 + i + 1) * 2 * width)
                other = jnp.concatenate([spread[:width, piece], spread[width:, piece]], axis=1)
                denom = row_term[at, :] - virt[:, cut]
                change = (own[at, :] + other) / denom
                out[at, cut] = (t[at, cut].astype(F32) + change).astype(BF16)


def local(amplitudes, integrals, irreps, occ_energy, virt_energy):
    _, occ_block, _, width, virt_total = amplitudes.shape
    lanes = occ_block * occ_block * width
    flat = amplitudes.reshape(lanes, virt_total)
    depth = integrals.shape[1]
    quarter = width // X
    npair = X * ZL * C
    index = lax.axis_index(PAIR)
    place = lax.axis_index(VIRT)
    t1 = passed_along(flat, "x", 1)
    t3 = passed_along(flat, "x", 3)

    pieces = spread(integrals, VIRT, NVIRT)
    labels_c = lax.dynamic_slice_in_dim(irreps, index * depth, depth)[:, None]
    labels_a = jnp.transpose(irreps.reshape(NVIRT, X, quarter), (1, 0, 2)).reshape(X, NVIRT * quarter)
    early, middle = lanes // 4, lanes * 5 // 8
    t2a = passed_along(t1[:early], "x", 1)
    pieces, t1, t3, t2a = lax.optimization_barrier((pieces, t1, t3, t2a))
    t2c = passed_along(t3[middle:], "x", 3)
    t2b = passed_along(t1[early:middle], "x", 1)
    sent = pl.pallas_call(
        turn_kernel,
        out_shape=jax.ShapeDtypeStruct((X * ZL, depth, NVIRT * quarter), BF16),
        in_specs=[VMEM] * 3,
        out_specs=VMEM,
        cost_estimate=pl.CostEstimate(flops=10_000_000, bytes_accessed=1_000_000, transcendentals=0),
        compiler_params=pltpu.CompilerParams(vmem_limit_bytes=12 * 2**20),
        name="turn",
    )(labels_c, labels_a, pieces)
    mine = lax.all_to_all(sent, ("x", "zl"), split_axis=0, concat_axis=0, tiled=True)
    mine, t2b, t2c = lax.optimization_barrier((mine, t2b, t2c))
    theirs = passed_along(mine, "c", 1)

    share = jax.ShapeDtypeStruct((NVIRT * quarter, lanes), BF16)
    mirror, own0, own1, own2, own3 = pl.pallas_call(
        cycle_kernel,
        out_shape=[jax.ShapeDtypeStruct((NVIRT, width, lanes), BF16)] + [share] * X,
        in_specs=[VMEM] * 8,
        out_specs=[VMEM] * 5,
        scratch_shapes=[
            pltpu.VMEM((virt_total, NVIRT * quarter), BF16),
            pltpu.VMEM((NVIRT * quarter, virt_total), BF16),
            pltpu.VMEM(flat.shape, BF16),
        ],
        cost_estimate=pl.CostEstimate(flops=1_210_000_000, bytes_accessed=6_000_000, transcendentals=0),
        compiler_params=pltpu.CompilerParams(vmem_limit_bytes=56 * 2**20),
        name="cycle",
    )(mine, theirs, flat, t1, t2a, t2b, t2c, t3)

    arrived = lax.all_to_all(
        mirror.reshape(NVIRT * X, quarter, lanes), VIRT + ("x",), split_axis=0, concat_axis=0, tiled=True
    ).reshape(NVIRT, width, lanes)
    own1 = passed_along(own1, "x", -1)
    own2 = passed_along(own2, "x", -2)
    own3 = passed_along(own3, "x", -3)

    partner = (index + npair // 2) % npair
    occ_i = lax.dynamic_slice_in_dim(occ_energy, index * occ_block, occ_block)
    occ_j = lax.dynamic_slice_in_dim(occ_energy, partner * occ_block, occ_block)
    virt_rows = lax.dynamic_slice_in_dim(virt_energy, place * width, width)
    row_term = (occ_i[:, None, None] + occ_j[None, :, None] - virt_rows[None, None, :]).reshape(lanes, 1)
    updated = pl.pallas_call(
        finish_kernel,
        out_shape=jax.ShapeDtypeStruct(flat.shape, BF16),
        in_specs=[VMEM] * 8,
        out_specs=VMEM,
        scratch_shapes=[pltpu.VMEM((NVIRT, width, lanes), BF16)],
        cost_estimate=pl.CostEstimate(flops=600_000_000, bytes_accessed=4_000_000, transcendentals=0),
        compiler_params=pltpu.CompilerParams(vmem_limit_bytes=12 * 2**20),
        name="finish",
    )(arrived, own0, own1, own2, own3, flat, row_term, virt_energy[None, :])
    return updated.reshape(amplitudes.shape)


def solution(mesh):
    fine = Mesh(mesh.devices.reshape(X, ZL, C, ZH, Y), PAIR + VIRT)
    placed = (P(PAIR, None, None, VIRT, None), P(VIRT, PAIR), P(), P(), P())
    return jax.shard_map(
        local,
        mesh=fine,
        in_specs=placed,
        out_specs=P(PAIR, None, None, VIRT, None),
        check_vma=False,
    )
```

```python
import jax
import jax.numpy as jnp
from jax import lax
from jax.experimental import pallas as pl
from jax.experimental.pallas import tpu as pltpu
from jax.sharding import Mesh, PartitionSpec as P

X, ZL, C = 4, 4, 2
ZH, Y = 3, 8
PAIR = ("x", "zl", "c")
VIRT = ("zh", "y")
NVIRT = ZH * Y
BF16, F32 = jnp.bfloat16, jnp.float32
VMEM = pl.BlockSpec(memory_space=pltpu.VMEM)
NT = (((1,), (1,)), ((), ()))


def passed_along(value, axis, steps):
    count = lax.axis_size(axis)
    pairs = [(source, (source + steps) % count) for source in range(count)]
    return lax.ppermute(value, axis, pairs)


def unit_matrix(size):
    rows = lax.broadcasted_iota(jnp.int32, (size, size), 0)
    return (rows == lax.broadcasted_iota(jnp.int32, (size, size), 1)).astype(BF16)


def spread(value, axis, count):
    copies = jnp.broadcast_to(value[None], (count,) + value.shape)
    return lax.all_to_all(copies, axis, split_axis=0, concat_axis=0, tiled=True)


def turn_kernel(labels_c, labels_a, pieces, out):
    depth = pieces.shape[2]
    quarter = pieces.shape[1] // X
    unit = unit_matrix(depth)
    for share in range(X):
        rows = pieces[:, share * quarter : (share + 1) * quarter, :].reshape(NVIRT * quarter, depth)
        turned = lax.dot_general(unit, rows, NT, preferred_element_type=F32)
        keep = labels_c[...] == labels_a[share : share + 1, :]
        masked = jnp.where(keep, turned, 0.0).astype(BF16)
        for copy in range(ZL):
            out[share * ZL + copy] = masked


def cycle_kernel(
    mine, theirs, t0, t1, t2a, t2b, t2c, t3, mirror, own0, own1, own2, own3, turned, held, t2
):
    x, c = lax.axis_index("x"), lax.axis_index("c")
    quarter = mirror.shape[1] // X
    count, depth, size = mine.shape
    for number in range(count):
        here = pl.multiple_of((2 * number + c) * depth, 16)
        there = pl.multiple_of((2 * number + 1 - c) * depth, 16)
        turned[pl.ds(here, depth), :] = mine[number]
        turned[pl.ds(there, depth), :] = theirs[number]
    unit = unit_matrix(size)
    for first in range(0, turned.shape[0], size):
        part = lax.dot_general(unit, turned[first : first + size, :], NT, preferred_element_type=F32)
        held[:, first : first + size] = part.astype(BF16)
    first = 0
    for part in (t2a, t2b, t2c):
        t2[first : first + part.shape[0], :] = part[...]
        first += part.shape[0]
    for steps, (t, own) in enumerate(((t0, own0), (t1, own1), (t2, own2), (t3, own3))):
        slot = lax.rem(x + (X + X // 2 - steps), X)
        value = lax.dot_general(held[...], t[...], NT, preferred_element_type=F32).astype(BF16)
        mirror[:, pl.ds(pl.multiple_of(slot * quarter, quarter), quarter), :] = value.reshape(
            NVIRT, quarter, value.shape[1]
        )
        own[...] = value


def finish_kernel(arrived, own0, own1, own2, own3, t, row_term, virt, out, own_rows):
    x = lax.axis_index("x")
    width, lanes = arrived.shape[1:]
    quarter = width // X
    pieces = lanes // width
    for steps, own in enumerate((own0, own1, own2, own3)):
        slot = lax.rem(x + steps, X)
        own_rows[:, pl.ds(pl.multiple_of(slot * quarter, quarter), quarter), :] = own[...].reshape(
            NVIRT, quarter, lanes
        )
    rows = lax.broadcasted_iota(jnp.int32, (lanes, lanes), 0)
    columns = lax.broadcasted_iota(jnp.int32, (lanes, lanes), 1)
    unit = (rows == columns).astype(BF16)
    rows = lax.broadcasted_iota(jnp.int32, (2 * lanes, 2 * lanes), 0)
    columns = lax.broadcasted_iota(jnp.int32, (2 * lanes, 2 * lanes), 1)
    odd, rest = rows // lanes, rows % lanes
    target = (rest // width) * (2 * width) + odd * width + rest % width
    moved = (columns == target).astype(BF16)
    for group in range(NVIRT // 4):
        cut = slice(group * 4 * width, (group + 1) * 4 * width)
        own = lax.dot_general(
            unit,
            own_rows[4 * group : 4 * group + 4].reshape(4 * width, lanes),
            NT,
            preferred_element_type=F32,
        )
        sent = [arrived[4 * group + k] for k in range(4)]
        stacked = jnp.concatenate(
            [
                jnp.concatenate([sent[0], sent[1]], axis=1),
                jnp.concatenate([sent[2], sent[3]], axis=1),
            ],
            axis=0,
        )
        spread = jnp.dot(stacked, moved, preferred_element_type=F32)
        for i in range(2):
            for j in range(2):
                at = slice((i * 2 + j) * width, (i * 2 + j + 1) * width)
                piece = slice((j * 2 + i) * 2 * width, (j * 2 + i + 1) * 2 * width)
                other = jnp.concatenate([spread[:width, piece], spread[width:, piece]], axis=1)
                denom = row_term[at, :] - virt[:, cut]
                change = (own[at, :] + other) / denom
                out[at, cut] = (t[at, cut].astype(F32) + change).astype(BF16)


def local(amplitudes, integrals, irreps, occ_energy, virt_energy):
    _, occ_block, _, width, virt_total = amplitudes.shape
    lanes = occ_block * occ_block * width
    flat = amplitudes.reshape(lanes, virt_total)
    depth = integrals.shape[1]
    quarter = width // X
    npair = X * ZL * C
    index = lax.axis_index(PAIR)
    place = lax.axis_index(VIRT)
    t1 = passed_along(flat, "x", 1)
    t3 = passed_along(flat, "x", 3)

    pieces = spread(integrals, VIRT, NVIRT)
    labels_c = lax.dynamic_slice_in_dim(irreps, index * depth, depth)[:, None]
    labels_a = jnp.transpose(irreps.reshape(NVIRT, X, quarter), (1, 0, 2)).reshape(X, NVIRT * quarter)
    early, middle = lanes // 8, lanes * 9 // 16
    t2a = passed_along(t1[:early], "x", 1)
    pieces, t1, t3, t2a = lax.optimization_barrier((pieces, t1, t3, t2a))
    t2c = passed_along(t3[middle:], "x", 3)
    t2b = passed_along(t1[early:middle], "x", 1)
    sent = pl.pallas_call(
        turn_kernel,
        out_shape=jax.ShapeDtypeStruct((X * ZL, depth, NVIRT * quarter), BF16),
        in_specs=[VMEM] * 3,
        out_specs=VMEM,
        cost_estimate=pl.CostEstimate(flops=10_000_000, bytes_accessed=1_000_000, transcendentals=0),
        compiler_params=pltpu.CompilerParams(vmem_limit_bytes=12 * 2**20),
        name="turn",
    )(labels_c, labels_a, pieces)
    mine = lax.all_to_all(sent, ("x", "zl"), split_axis=0, concat_axis=0, tiled=True)
    mine, t2b, t2c = lax.optimization_barrier((mine, t2b, t2c))
    theirs = passed_along(mine, "c", 1)

    share = jax.ShapeDtypeStruct((NVIRT * quarter, lanes), BF16)
    mirror, own0, own1, own2, own3 = pl.pallas_call(
        cycle_kernel,
        out_shape=[jax.ShapeDtypeStruct((NVIRT, width, lanes), BF16)] + [share] * X,
        in_specs=[VMEM] * 8,
        out_specs=[VMEM] * 5,
        scratch_shapes=[
            pltpu.VMEM((virt_total, NVIRT * quarter), BF16),
            pltpu.VMEM((NVIRT * quarter, virt_total), BF16),
            pltpu.VMEM(flat.shape, BF16),
        ],
        cost_estimate=pl.CostEstimate(flops=1_210_000_000, bytes_accessed=6_000_000, transcendentals=0),
        compiler_params=pltpu.CompilerParams(vmem_limit_bytes=56 * 2**20),
        name="cycle",
    )(mine, theirs, flat, t1, t2a, t2b, t2c, t3)

    arrived = lax.all_to_all(
        mirror.reshape(NVIRT * X, quarter, lanes), VIRT + ("x",), split_axis=0, concat_axis=0, tiled=True
    ).reshape(NVIRT, width, lanes)
    own1 = passed_along(own1, "x", -1)
    own2 = passed_along(own2, "x", -2)
    own3 = passed_along(own3, "x", -3)

    partner = (index + npair // 2) % npair
    occ_i = lax.dynamic_slice_in_dim(occ_energy, index * occ_block, occ_block)
    occ_j = lax.dynamic_slice_in_dim(occ_energy, partner * occ_block, occ_block)
    virt_rows = lax.dynamic_slice_in_dim(virt_energy, place * width, width)
    row_term = (occ_i[:, None, None] + occ_j[None, :, None] - virt_rows[None, None, :]).reshape(lanes, 1)
    updated = pl.pallas_call(
        finish_kernel,
        out_shape=jax.ShapeDtypeStruct(flat.shape, BF16),
        in_specs=[VMEM] * 8,
        out_specs=VMEM,
        scratch_shapes=[pltpu.VMEM((NVIRT, width, lanes), BF16)],
        cost_estimate=pl.CostEstimate(flops=600_000_000, bytes_accessed=4_000_000, transcendentals=0),
        compiler_params=pltpu.CompilerParams(vmem_limit_bytes=12 * 2**20),
        name="finish",
    )(arrived, own0, own1, own2, own3, flat, row_term, virt_energy[None, :])
    return updated.reshape(amplitudes.shape)


def solution(mesh):
    fine = Mesh(mesh.devices.reshape(X, ZL, C, ZH, Y), PAIR + VIRT)
    placed = (P(PAIR, None, None, VIRT, None), P(VIRT, PAIR), P(), P(), P())
    return jax.shard_map(
        local,
        mesh=fine,
        in_specs=placed,
        out_specs=P(PAIR, None, None, VIRT, None),
        check_vma=False,
    )
```

```python
import jax
import jax.numpy as jnp
from jax import lax
from jax.experimental import pallas as pl
from jax.experimental.pallas import tpu as pltpu
from jax.sharding import Mesh, PartitionSpec as P

X, ZL, C = 4, 4, 2
ZH, Y = 3, 8
PAIR = ("x", "zl", "c")
VIRT = ("zh", "y")
NVIRT = ZH * Y
BF16, F32 = jnp.bfloat16, jnp.float32
VMEM = pl.BlockSpec(memory_space=pltpu.VMEM)
NT = (((1,), (1,)), ((), ()))


def passed_along(value, axis, steps):
    count = lax.axis_size(axis)
    pairs = [(source, (source + steps) % count) for source in range(count)]
    return lax.ppermute(value, axis, pairs)


def unit_matrix(size):
    rows = lax.broadcasted_iota(jnp.int32, (size, size), 0)
    return (rows == lax.broadcasted_iota(jnp.int32, (size, size), 1)).astype(BF16)


def spread(value, axis, count):
    copies = jnp.broadcast_to(value[None], (count,) + value.shape)
    return lax.all_to_all(copies, axis, split_axis=0, concat_axis=0, tiled=True)


def turn_kernel(labels_c, labels_a, pieces, out):
    depth = pieces.shape[2]
    quarter = pieces.shape[1] // X
    unit = unit_matrix(depth)
    for share in range(X):
        rows = pieces[:, share * quarter : (share + 1) * quarter, :].reshape(NVIRT * quarter, depth)
        turned = lax.dot_general(unit, rows, NT, preferred_element_type=F32)
        keep = labels_c[...] == labels_a[share : share + 1, :]
        masked = jnp.where(keep, turned, 0.0).astype(BF16)
        for copy in range(ZL):
            out[share * ZL + copy] = masked


def cycle_kernel(
    mine, theirs, t0, t1, t2a, t2b, t2c, t3, mirror, own0, own1, own2, own3, turned, held, t2
):
    x, c = lax.axis_index("x"), lax.axis_index("c")
    quarter = mirror.shape[1] // X
    count, depth, size = mine.shape
    for number in range(count):
        here = pl.multiple_of((2 * number + c) * depth, 16)
        there = pl.multiple_of((2 * number + 1 - c) * depth, 16)
        turned[pl.ds(here, depth), :] = mine[number]
        turned[pl.ds(there, depth), :] = theirs[number]
    unit = unit_matrix(size)
    for first in range(0, turned.shape[0], size):
        part = lax.dot_general(unit, turned[first : first + size, :], NT, preferred_element_type=F32)
        held[:, first : first + size] = part.astype(BF16)
    first = 0
    for part in (t2a, t2b, t2c):
        t2[first : first + part.shape[0], :] = part[...]
        first += part.shape[0]
    for steps, (t, own) in enumerate(((t0, own0), (t1, own1), (t2, own2), (t3, own3))):
        slot = lax.rem(x + (X + X // 2 - steps), X)
        value = lax.dot_general(held[...], t[...], NT, preferred_element_type=F32).astype(BF16)
        mirror[:, pl.ds(pl.multiple_of(slot * quarter, quarter), quarter), :] = value.reshape(
            NVIRT, quarter, value.shape[1]
        )
        own[...] = value


def finish_kernel(arrived, own0, own1, own2, own3, t, row_term, virt, out, own_rows):
    x = lax.axis_index("x")
    width, lanes = arrived.shape[1:]
    quarter = width // X
    pieces = lanes // width
    for steps, own in enumerate((own0, own1, own2, own3)):
        slot = lax.rem(x + steps, X)
        own_rows[:, pl.ds(pl.multiple_of(slot * quarter, quarter), quarter), :] = own[...].reshape(
            NVIRT, quarter, lanes
        )
    rows = lax.broadcasted_iota(jnp.int32, (lanes, lanes), 0)
    columns = lax.broadcasted_iota(jnp.int32, (lanes, lanes), 1)
    unit = (rows == columns).astype(BF16)
    rows = lax.broadcasted_iota(jnp.int32, (2 * lanes, 2 * lanes), 0)
    columns = lax.broadcasted_iota(jnp.int32, (2 * lanes, 2 * lanes), 1)
    odd, rest = rows // lanes, rows % lanes
    target = (rest // width) * (2 * width) + odd * width + rest % width
    moved = (columns == target).astype(BF16)
    for group in range(NVIRT // 4):
        cut = slice(group * 4 * width, (group + 1) * 4 * width)
        own = lax.dot_general(
            unit,
            own_rows[4 * group : 4 * group + 4].reshape(4 * width, lanes),
            NT,
            preferred_element_type=F32,
        )
        sent = [arrived[4 * group + k] for k in range(4)]
        stacked = jnp.concatenate(
            [
                jnp.concatenate([sent[0], sent[1]], axis=1),
                jnp.concatenate([sent[2], sent[3]], axis=1),
            ],
            axis=0,
        )
        spread = jnp.dot(stacked, moved, preferred_element_type=F32)
        for i in range(2):
            for j in range(2):
                at = slice((i * 2 + j) * width, (i * 2 + j + 1) * width)
                piece = slice((j * 2 + i) * 2 * width, (j * 2 + i + 1) * 2 * width)
                other = jnp.concatenate([spread[:width, piece], spread[width:, piece]], axis=1)
                denom = row_term[at, :] - virt[:, cut]
                change = (own[at, :] + other) / denom
                out[at, cut] = (t[at, cut].astype(F32) + change).astype(BF16)


def local(amplitudes, integrals, irreps, occ_energy, virt_energy):
    _, occ_block, _, width, virt_total = amplitudes.shape
    lanes = occ_block * occ_block * width
    flat = amplitudes.reshape(lanes, virt_total)
    depth = integrals.shape[1]
    quarter = width // X
    npair = X * ZL * C
    index = lax.axis_index(PAIR)
    place = lax.axis_index(VIRT)
    t1 = passed_along(flat, "x", 1)
    t3 = passed_along(flat, "x", 3)

    pieces = spread(integrals.reshape(2, -1), VIRT, NVIRT).reshape(NVIRT, width, depth)
    labels_c = lax.dynamic_slice_in_dim(irreps, index * depth, depth)[:, None]
    labels_a = jnp.transpose(irreps.reshape(NVIRT, X, quarter), (1, 0, 2)).reshape(X, NVIRT * quarter)
    early, middle = lanes // 8, lanes * 9 // 16
    t2a = passed_along(t1[:early], "x", 1)
    pieces, t1, t3, t2a = lax.optimization_barrier((pieces, t1, t3, t2a))
    t2c = passed_along(t3[middle:], "x", 3)
    t2b = passed_along(t1[early:middle], "x", 1)
    sent = pl.pallas_call(
        turn_kernel,
        out_shape=jax.ShapeDtypeStruct((X * ZL, depth, NVIRT * quarter), BF16),
        in_specs=[VMEM] * 3,
        out_specs=VMEM,
        cost_estimate=pl.CostEstimate(flops=10_000_000, bytes_accessed=1_000_000, transcendentals=0),
        compiler_params=pltpu.CompilerParams(vmem_limit_bytes=12 * 2**20),
        name="turn",
    )(labels_c, labels_a, pieces)
    mine = lax.all_to_all(sent, ("x", "zl"), split_axis=0, concat_axis=0, tiled=True)
    mine, t2b, t2c = lax.optimization_barrier((mine, t2b, t2c))
    theirs = passed_along(mine, "c", 1)

    share = jax.ShapeDtypeStruct((NVIRT * quarter, lanes), BF16)
    mirror, own0, own1, own2, own3 = pl.pallas_call(
        cycle_kernel,
        out_shape=[jax.ShapeDtypeStruct((NVIRT, width, lanes), BF16)] + [share] * X,
        in_specs=[VMEM] * 8,
        out_specs=[VMEM] * 5,
        scratch_shapes=[
            pltpu.VMEM((virt_total, NVIRT * quarter), BF16),
            pltpu.VMEM((NVIRT * quarter, virt_total), BF16),
            pltpu.VMEM(flat.shape, BF16),
        ],
        cost_estimate=pl.CostEstimate(flops=1_210_000_000, bytes_accessed=6_000_000, transcendentals=0),
        compiler_params=pltpu.CompilerParams(vmem_limit_bytes=56 * 2**20),
        name="cycle",
    )(mine, theirs, flat, t1, t2a, t2b, t2c, t3)

    arrived = lax.all_to_all(
        mirror.reshape(NVIRT * X, quarter, lanes), VIRT + ("x",), split_axis=0, concat_axis=0, tiled=True
    ).reshape(NVIRT, width, lanes)
    own1 = passed_along(own1, "x", -1)
    own2 = passed_along(own2, "x", -2)
    own3 = passed_along(own3, "x", -3)

    partner = (index + npair // 2) % npair
    occ_i = lax.dynamic_slice_in_dim(occ_energy, index * occ_block, occ_block)
    occ_j = lax.dynamic_slice_in_dim(occ_energy, partner * occ_block, occ_block)
    virt_rows = lax.dynamic_slice_in_dim(virt_energy, place * width, width)
    row_term = (occ_i[:, None, None] + occ_j[None, :, None] - virt_rows[None, None, :]).reshape(lanes, 1)
    updated = pl.pallas_call(
        finish_kernel,
        out_shape=jax.ShapeDtypeStruct(flat.shape, BF16),
        in_specs=[VMEM] * 8,
        out_specs=VMEM,
        scratch_shapes=[pltpu.VMEM((NVIRT, width, lanes), BF16)],
        cost_estimate=pl.CostEstimate(flops=600_000_000, bytes_accessed=4_000_000, transcendentals=0),
        compiler_params=pltpu.CompilerParams(vmem_limit_bytes=12 * 2**20),
        name="finish",
    )(arrived, own0, own1, own2, own3, flat, row_term, virt_energy[None, :])
    return updated.reshape(amplitudes.shape)


def solution(mesh):
    fine = Mesh(mesh.devices.reshape(X, ZL, C, ZH, Y), PAIR + VIRT)
    placed = (P(PAIR, None, None, VIRT, None), P(VIRT, PAIR), P(), P(), P())
    return jax.shard_map(
        local,
        mesh=fine,
        in_specs=placed,
        out_specs=P(PAIR, None, None, VIRT, None),
        check_vma=False,
    )
```

```python
import jax
import jax.numpy as jnp
from jax import lax
from jax.experimental import pallas as pl
from jax.experimental.pallas import tpu as pltpu
from jax.sharding import Mesh, PartitionSpec as P

X, ZL, C = 4, 4, 2
ZH, Y = 3, 8
PAIR = ("x", "zl", "c")
VIRT = ("zh", "y")
NVIRT = ZH * Y
BF16, F32 = jnp.bfloat16, jnp.float32
VMEM = pl.BlockSpec(memory_space=pltpu.VMEM)
NT = (((1,), (1,)), ((), ()))


def passed_along(value, axis, steps):
    count = lax.axis_size(axis)
    pairs = [(source, (source + steps) % count) for source in range(count)]
    return lax.ppermute(value, axis, pairs)


def unit_matrix(size):
    rows = lax.broadcasted_iota(jnp.int32, (size, size), 0)
    return (rows == lax.broadcasted_iota(jnp.int32, (size, size), 1)).astype(BF16)


def spread(value, axis, count):
    copies = jnp.broadcast_to(value[None], (count,) + value.shape)
    return lax.all_to_all(copies, axis, split_axis=0, concat_axis=0, tiled=True)


def turn_kernel(labels_c, labels_a, pieces, out):
    depth = pieces.shape[2]
    quarter = pieces.shape[1] // X
    unit = unit_matrix(depth)
    for share in range(X):
        rows = pieces[:, share * quarter : (share + 1) * quarter, :].reshape(NVIRT * quarter, depth)
        turned = lax.dot_general(unit, rows, NT, preferred_element_type=F32)
        keep = labels_c[...] == labels_a[share : share + 1, :]
        masked = jnp.where(keep, turned, 0.0).astype(BF16)
        for copy in range(ZL):
            out[share * ZL + copy] = masked


def cycle_kernel(
    mine, theirs, t0, t1, t2a, t2b, t2c, t3, mirror, own0, own1, own2, own3, turned, held, t2
):
    x, c = lax.axis_index("x"), lax.axis_index("c")
    quarter = mirror.shape[1] // X
    count, depth, size = mine.shape
    for number in range(count):
        here = pl.multiple_of((2 * number + c) * depth, 16)
        there = pl.multiple_of((2 * number + 1 - c) * depth, 16)
        turned[pl.ds(here, depth), :] = mine[number]
        turned[pl.ds(there, depth), :] = theirs[number]
    unit = unit_matrix(size)
    for first in range(0, turned.shape[0], size):
        part = lax.dot_general(unit, turned[first : first + size, :], NT, preferred_element_type=F32)
        held[:, first : first + size] = part.astype(BF16)
    first = 0
    for part in (t2a, t2b, t2c):
        t2[first : first + part.shape[0], :] = part[...]
        first += part.shape[0]
    for steps, (t, own) in enumerate(((t0, own0), (t1, own1), (t2, own2), (t3, own3))):
        slot = lax.rem(x + (X + X // 2 - steps), X)
        value = lax.dot_general(held[...], t[...], NT, preferred_element_type=F32).astype(BF16)
        mirror[:, pl.ds(pl.multiple_of(slot * quarter, quarter), quarter), :] = value.reshape(
            NVIRT, quarter, value.shape[1]
        )
        own[...] = value


def finish_kernel(arrived, own0, own1, own2, own3, t, row_term, virt, out, own_rows):
    x = lax.axis_index("x")
    width, lanes = arrived.shape[1:]
    quarter = width // X
    pieces = lanes // width
    for steps, own in enumerate((own0, own1, own2, own3)):
        slot = lax.rem(x + steps, X)
        own_rows[:, pl.ds(pl.multiple_of(slot * quarter, quarter), quarter), :] = own[...].reshape(
            NVIRT, quarter, lanes
        )
    rows = lax.broadcasted_iota(jnp.int32, (lanes, lanes), 0)
    columns = lax.broadcasted_iota(jnp.int32, (lanes, lanes), 1)
    unit = (rows == columns).astype(BF16)
    rows = lax.broadcasted_iota(jnp.int32, (2 * lanes, 2 * lanes), 0)
    columns = lax.broadcasted_iota(jnp.int32, (2 * lanes, 2 * lanes), 1)
    odd, rest = rows // lanes, rows % lanes
    target = (rest // width) * (2 * width) + odd * width + rest % width
    moved = (columns == target).astype(BF16)
    for group in range(NVIRT // 4):
        cut = slice(group * 4 * width, (group + 1) * 4 * width)
        own = lax.dot_general(
            unit,
            own_rows[4 * group : 4 * group + 4].reshape(4 * width, lanes),
            NT,
            preferred_element_type=F32,
        )
        sent = [arrived[4 * group + k] for k in range(4)]
        stacked = jnp.concatenate(
            [
                jnp.concatenate([sent[0], sent[1]], axis=1),
                jnp.concatenate([sent[2], sent[3]], axis=1),
            ],
            axis=0,
        )
        spread = jnp.dot(stacked, moved, preferred_element_type=F32)
        for i in range(2):
            for j in range(2):
                at = slice((i * 2 + j) * width, (i * 2 + j + 1) * width)
                piece = slice((j * 2 + i) * 2 * width, (j * 2 + i + 1) * 2 * width)
                other = jnp.concatenate([spread[:width, piece], spread[width:, piece]], axis=1)
                denom = row_term[at, :] - virt[:, cut]
                change = (own[at, :] + other) / denom
                out[at, cut] = (t[at, cut].astype(F32) + change).astype(BF16)


def local(amplitudes, integrals, irreps, occ_energy, virt_energy):
    _, occ_block, _, width, virt_total = amplitudes.shape
    lanes = occ_block * occ_block * width
    flat = amplitudes.reshape(lanes, virt_total)
    depth = integrals.shape[1]
    quarter = width // X
    npair = X * ZL * C
    index = lax.axis_index(PAIR)
    place = lax.axis_index(VIRT)
    t1 = passed_along(flat, "x", 1)
    t3 = passed_along(flat, "x", 3)

    pieces = spread(integrals.reshape(-1, 128), VIRT, NVIRT).reshape(NVIRT, width, depth)
    labels_c = lax.dynamic_slice_in_dim(irreps, index * depth, depth)[:, None]
    labels_a = jnp.transpose(irreps.reshape(NVIRT, X, quarter), (1, 0, 2)).reshape(X, NVIRT * quarter)
    early, middle = lanes // 8, lanes * 9 // 16
    t2a = passed_along(t1[:early], "x", 1)
    pieces, t1, t3, t2a = lax.optimization_barrier((pieces, t1, t3, t2a))
    t2c = passed_along(t3[middle:], "x", 3)
    t2b = passed_along(t1[early:middle], "x", 1)
    sent = pl.pallas_call(
        turn_kernel,
        out_shape=jax.ShapeDtypeStruct((X * ZL, depth, NVIRT * quarter), BF16),
        in_specs=[VMEM] * 3,
        out_specs=VMEM,
        cost_estimate=pl.CostEstimate(flops=10_000_000, bytes_accessed=1_000_000, transcendentals=0),
        compiler_params=pltpu.CompilerParams(vmem_limit_bytes=12 * 2**20),
        name="turn",
    )(labels_c, labels_a, pieces)
    mine = lax.all_to_all(sent, ("x", "zl"), split_axis=0, concat_axis=0, tiled=True)
    mine, t2b, t2c = lax.optimization_barrier((mine, t2b, t2c))
    theirs = passed_along(mine, "c", 1)

    share = jax.ShapeDtypeStruct((NVIRT * quarter, lanes), BF16)
    mirror, own0, own1, own2, own3 = pl.pallas_call(
        cycle_kernel,
        out_shape=[jax.ShapeDtypeStruct((NVIRT, width, lanes), BF16)] + [share] * X,
        in_specs=[VMEM] * 8,
        out_specs=[VMEM] * 5,
        scratch_shapes=[
            pltpu.VMEM((virt_total, NVIRT * quarter), BF16),
            pltpu.VMEM((NVIRT * quarter, virt_total), BF16),
            pltpu.VMEM(flat.shape, BF16),
        ],
        cost_estimate=pl.CostEstimate(flops=1_210_000_000, bytes_accessed=6_000_000, transcendentals=0),
        compiler_params=pltpu.CompilerParams(vmem_limit_bytes=56 * 2**20),
        name="cycle",
    )(mine, theirs, flat, t1, t2a, t2b, t2c, t3)

    arrived = lax.all_to_all(
        mirror.reshape(NVIRT * X, quarter, lanes), VIRT + ("x",), split_axis=0, concat_axis=0, tiled=True
    ).reshape(NVIRT, width, lanes)
    own1 = passed_along(own1, "x", -1)
    own2 = passed_along(own2, "x", -2)
    own3 = passed_along(own3, "x", -3)

    partner = (index + npair // 2) % npair
    occ_i = lax.dynamic_slice_in_dim(occ_energy, index * occ_block, occ_block)
    occ_j = lax.dynamic_slice_in_dim(occ_energy, partner * occ_block, occ_block)
    virt_rows = lax.dynamic_slice_in_dim(virt_energy, place * width, width)
    row_term = (occ_i[:, None, None] + occ_j[None, :, None] - virt_rows[None, None, :]).reshape(lanes, 1)
    updated = pl.pallas_call(
        finish_kernel,
        out_shape=jax.ShapeDtypeStruct(flat.shape, BF16),
        in_specs=[VMEM] * 8,
        out_specs=VMEM,
        scratch_shapes=[pltpu.VMEM((NVIRT, width, lanes), BF16)],
        cost_estimate=pl.CostEstimate(flops=600_000_000, bytes_accessed=4_000_000, transcendentals=0),
        compiler_params=pltpu.CompilerParams(vmem_limit_bytes=12 * 2**20),
        name="finish",
    )(arrived, own0, own1, own2, own3, flat, row_term, virt_energy[None, :])
    return updated.reshape(amplitudes.shape)


def solution(mesh):
    fine = Mesh(mesh.devices.reshape(X, ZL, C, ZH, Y), PAIR + VIRT)
    placed = (P(PAIR, None, None, VIRT, None), P(VIRT, PAIR), P(), P(), P())
    return jax.shard_map(
        local,
        mesh=fine,
        in_specs=placed,
        out_specs=P(PAIR, None, None, VIRT, None),
        check_vma=False,
    )
```

```python
import jax
import jax.numpy as jnp
from jax import lax
from jax.experimental import pallas as pl
from jax.experimental.pallas import tpu as pltpu
from jax.sharding import Mesh, PartitionSpec as P

X, ZL, C = 4, 4, 2
ZH, Y = 3, 8
PAIR = ("x", "zl", "c")
VIRT = ("zh", "y")
NVIRT = ZH * Y
BF16, F32 = jnp.bfloat16, jnp.float32
VMEM = pl.BlockSpec(memory_space=pltpu.VMEM)
NT = (((1,), (1,)), ((), ()))


def passed_along(value, axis, steps):
    count = lax.axis_size(axis)
    pairs = [(source, (source + steps) % count) for source in range(count)]
    return lax.ppermute(value, axis, pairs)


def unit_matrix(size):
    rows = lax.broadcasted_iota(jnp.int32, (size, size), 0)
    return (rows == lax.broadcasted_iota(jnp.int32, (size, size), 1)).astype(BF16)


def spread(value, axis, count):
    copies = jnp.broadcast_to(value[None], (count,) + value.shape)
    return lax.all_to_all(copies, axis, split_axis=0, concat_axis=0, tiled=True)


def turn_kernel(labels_c, labels_a, pieces, out):
    depth = pieces.shape[2]
    quarter = pieces.shape[1] // X
    unit = unit_matrix(depth)
    for share in range(X):
        rows = pieces[:, share * quarter : (share + 1) * quarter, :].reshape(NVIRT * quarter, depth)
        turned = lax.dot_general(unit, rows, NT, preferred_element_type=F32)
        keep = labels_c[...] == labels_a[share : share + 1, :]
        masked = jnp.where(keep, turned, 0.0).astype(BF16)
        for copy in range(ZL):
            out[share * ZL + copy] = masked


def cycle_kernel(
    mine, theirs, t0, t1, t2a, t2b, t2c, t3, mirror, own0, own1, own2, own3, turned, held, t2
):
    x, c = lax.axis_index("x"), lax.axis_index("c")
    quarter = mirror.shape[1] // X
    count, depth, size = mine.shape
    for number in range(count):
        here = pl.multiple_of((2 * number + c) * depth, 16)
        there = pl.multiple_of((2 * number + 1 - c) * depth, 16)
        turned[pl.ds(here, depth), :] = mine[number]
        turned[pl.ds(there, depth), :] = theirs[number]
    unit = unit_matrix(size)
    for first in range(0, turned.shape[0], size):
        part = lax.dot_general(unit, turned[first : first + size, :], NT, preferred_element_type=F32)
        held[:, first : first + size] = part.astype(BF16)
    first = 0
    for part in (t2a, t2b, t2c):
        t2[first : first + part.shape[0], :] = part[...]
        first += part.shape[0]
    for steps, (t, own) in enumerate(((t0, own0), (t1, own1), (t2, own2), (t3, own3))):
        slot = lax.rem(x + (X + X // 2 - steps), X)
        value = lax.dot_general(held[...], t[...], NT, preferred_element_type=F32).astype(BF16)
        mirror[:, pl.ds(pl.multiple_of(slot * quarter, quarter), quarter), :] = value.reshape(
            NVIRT, quarter, value.shape[1]
        )
        own[...] = value


def finish_kernel(arrived, own0, own1, own2, own3, t, row_term, virt, out, own_rows):
    x = lax.axis_index("x")
    width, lanes = arrived.shape[1:]
    quarter = width // X
    pieces = lanes // width
    for steps, own in enumerate((own0, own1, own2, own3)):
        slot = lax.rem(x + steps, X)
        own_rows[:, pl.ds(pl.multiple_of(slot * quarter, quarter), quarter), :] = own[...].reshape(
            NVIRT, quarter, lanes
        )
    rows = lax.broadcasted_iota(jnp.int32, (lanes, lanes), 0)
    columns = lax.broadcasted_iota(jnp.int32, (lanes, lanes), 1)
    unit = (rows == columns).astype(BF16)
    rows = lax.broadcasted_iota(jnp.int32, (2 * lanes, 2 * lanes), 0)
    columns = lax.broadcasted_iota(jnp.int32, (2 * lanes, 2 * lanes), 1)
    odd, rest = rows // lanes, rows % lanes
    target = (rest // width) * (2 * width) + odd * width + rest % width
    moved = (columns == target).astype(BF16)
    for group in range(NVIRT // 4):
        cut = slice(group * 4 * width, (group + 1) * 4 * width)
        own = lax.dot_general(
            unit,
            own_rows[4 * group : 4 * group + 4].reshape(4 * width, lanes),
            NT,
            preferred_element_type=F32,
        )
        sent = [arrived[4 * group + k] for k in range(4)]
        stacked = jnp.concatenate(
            [
                jnp.concatenate([sent[0], sent[1]], axis=1),
                jnp.concatenate([sent[2], sent[3]], axis=1),
            ],
            axis=0,
        )
        spread = jnp.dot(stacked, moved, preferred_element_type=F32)
        for i in range(2):
            for j in range(2):
                at = slice((i * 2 + j) * width, (i * 2 + j + 1) * width)
                piece = slice((j * 2 + i) * 2 * width, (j * 2 + i + 1) * 2 * width)
                other = jnp.concatenate([spread[:width, piece], spread[width:, piece]], axis=1)
                denom = row_term[at, :] - virt[:, cut]
                change = (own[at, :] + other) / denom
                out[at, cut] = (t[at, cut].astype(F32) + change).astype(BF16)


def local(amplitudes, integrals, irreps, occ_energy, virt_energy):
    _, occ_block, _, width, virt_total = amplitudes.shape
    lanes = occ_block * occ_block * width
    flat = amplitudes.reshape(lanes, virt_total)
    depth = integrals.shape[1]
    quarter = width // X
    npair = X * ZL * C
    index = lax.axis_index(PAIR)
    place = lax.axis_index(VIRT)
    t1 = passed_along(flat, "x", 1)
    t3 = passed_along(flat, "x", 3)

    pieces = spread(integrals.reshape(2, -1), VIRT, NVIRT).reshape(NVIRT, width, depth)
    labels_c = lax.dynamic_slice_in_dim(irreps, index * depth, depth)[:, None]
    labels_a = jnp.transpose(irreps.reshape(NVIRT, X, quarter), (1, 0, 2)).reshape(X, NVIRT * quarter)
    early, middle = lanes // 8, lanes * 5 // 8
    t2a = passed_along(t1[:early], "x", 1)
    pieces, t1, t3, t2a = lax.optimization_barrier((pieces, t1, t3, t2a))
    t2c = passed_along(t3[middle:], "x", 3)
    t2b = passed_along(t1[early:middle], "x", 1)
    sent = pl.pallas_call(
        turn_kernel,
        out_shape=jax.ShapeDtypeStruct((X * ZL, depth, NVIRT * quarter), BF16),
        in_specs=[VMEM] * 3,
        out_specs=VMEM,
        cost_estimate=pl.CostEstimate(flops=10_000_000, bytes_accessed=1_000_000, transcendentals=0),
        compiler_params=pltpu.CompilerParams(vmem_limit_bytes=12 * 2**20),
        name="turn",
    )(labels_c, labels_a, pieces)
    mine = lax.all_to_all(sent, ("x", "zl"), split_axis=0, concat_axis=0, tiled=True)
    mine, t2b, t2c = lax.optimization_barrier((mine, t2b, t2c))
    theirs = passed_along(mine, "c", 1)

    share = jax.ShapeDtypeStruct((NVIRT * quarter, lanes), BF16)
    mirror, own0, own1, own2, own3 = pl.pallas_call(
        cycle_kernel,
        out_shape=[jax.ShapeDtypeStruct((NVIRT, width, lanes), BF16)] + [share] * X,
        in_specs=[VMEM] * 8,
        out_specs=[VMEM] * 5,
        scratch_shapes=[
            pltpu.VMEM((virt_total, NVIRT * quarter), BF16),
            pltpu.VMEM((NVIRT * quarter, virt_total), BF16),
            pltpu.VMEM(flat.shape, BF16),
        ],
        cost_estimate=pl.CostEstimate(flops=1_210_000_000, bytes_accessed=6_000_000, transcendentals=0),
        compiler_params=pltpu.CompilerParams(vmem_limit_bytes=56 * 2**20),
        name="cycle",
    )(mine, theirs, flat, t1, t2a, t2b, t2c, t3)

    arrived = lax.all_to_all(
        mirror.reshape(NVIRT * X, quarter, lanes), VIRT + ("x",), split_axis=0, concat_axis=0, tiled=True
    ).reshape(NVIRT, width, lanes)
    own1 = passed_along(own1, "x", -1)
    own2 = passed_along(own2, "x", -2)
    own3 = passed_along(own3, "x", -3)

    partner = (index + npair // 2) % npair
    occ_i = lax.dynamic_slice_in_dim(occ_energy, index * occ_block, occ_block)
    occ_j = lax.dynamic_slice_in_dim(occ_energy, partner * occ_block, occ_block)
    virt_rows = lax.dynamic_slice_in_dim(virt_energy, place * width, width)
    row_term = (occ_i[:, None, None] + occ_j[None, :, None] - virt_rows[None, None, :]).reshape(lanes, 1)
    updated = pl.pallas_call(
        finish_kernel,
        out_shape=jax.ShapeDtypeStruct(flat.shape, BF16),
        in_specs=[VMEM] * 8,
        out_specs=VMEM,
        scratch_shapes=[pltpu.VMEM((NVIRT, width, lanes), BF16)],
        cost_estimate=pl.CostEstimate(flops=600_000_000, bytes_accessed=4_000_000, transcendentals=0),
        compiler_params=pltpu.CompilerParams(vmem_limit_bytes=12 * 2**20),
        name="finish",
    )(arrived, own0, own1, own2, own3, flat, row_term, virt_energy[None, :])
    return updated.reshape(amplitudes.shape)


def solution(mesh):
    fine = Mesh(mesh.devices.reshape(X, ZL, C, ZH, Y), PAIR + VIRT)
    placed = (P(PAIR, None, None, VIRT, None), P(VIRT, PAIR), P(), P(), P())
    return jax.shard_map(
        local,
        mesh=fine,
        in_specs=placed,
        out_specs=P(PAIR, None, None, VIRT, None),
        check_vma=False,
    )
```
